1024 devices in a mesh: wide: 128 (over y, z, core), narrow: 8 (over x).
Axes of the slice: x: 8, y: 8, z: 8, core: 2. Of those that a mesh axis runs over, the one named last changes fastest.
Arguments:
- tokens: bfloat16 [4096, 4096], P('wide', 'narrow'), may hold values from -6 to 6
- cotangent: bfloat16 [4096, 4096], P('wide', 'narrow'), may hold values from -6 to 6
- gate_logits: float32 [4096, 4], P('wide'), may hold values from -6 to 6
- node_groups: int32 [4096, 4], P('wide'), may hold values from 0 to 127, all different within a row; in each aligned block of 32 rows (0 to 31, 32 to 63, ...) at most 2 rows name the same one
- sample_ids: int32 [4096], P('wide'), may hold values from 0 to 63
- advantages: float32 [64], replicated, may hold values from -4 to 4
- up_weight: bfloat16 [128, 4096, 1024], P('wide', 'narrow'), may hold values from -0.09375 to 0.09375
- down_weight: bfloat16 [128, 1024, 4096], P('wide', None, 'narrow'), may hold values from -0.1875 to 0.1875
Outputs:
- mixed: bfloat16 [4096, 4096], P('wide', 'narrow')
- token_grad: bfloat16 [4096, 4096], P('wide', 'narrow')
- logit_grad: float32 [4096, 4], P('wide')
The draws below stay inside these ranges and needn't reach their ends.
Inputs may be any that keep to these rules, and one draw needn't show every extreme that they name: `node_groups`: the 4 node groups of a token are distinct. Among the tokens of one index of wide (aligned blocks of 32 tokens), at most 2 name any one node group, and some node group is named by exactly 2 of them.
All inputs are finite; a program needn't handle non-finite values.
Results may differ from the reference program's by a relative error of at most 0.034.
Values may be sent and summed in bfloat16 or wider, within the bound.
A program may use at most 32 MiB of HBM per device.

```python
import math
import jax
import jax.numpy as jnp
import numpy as np
from jax import lax

D = 4096
FF = 1024
PICKS = 4
SAMPLES = 64
TOK_GROUP = 32
EXPERTS = 128
TOKENS = 4096
CAP = 2
N_WIDE = 128
N_NARROW = 8


def with_ends(entries, rng, smallest, high):
    spot = [jax.random.randint(jax.random.fold_in(rng, axis), (), 0, length) for axis, length in enumerate(entries.shape)]
    longest = entries.shape.index(max(entries.shape))
    neighbour = spot[:longest] + [(spot[longest] + 1) % entries.shape[longest]] + spot[longest + 1:]
    return entries.at[tuple(spot)].set(smallest).at[tuple(neighbour)].set(high)


def block_scale(rng, extent, cuts, low, largest):
    def one(dim, shards_of):
        draws = jax.random.uniform(jax.random.fold_in(jax.random.fold_in(rng, 6), dim), (shards_of,), jnp.float32, low / len(cuts), largest / len(cuts))
        return jnp.repeat(jnp.exp(draws), extent[dim] // shards_of).reshape((-1,) + (1,) * (len(extent) - dim - 1))

    factor_of = one(*cuts[0])
    for cut in cuts[1:]:
        factor_of = factor_of * one(*cut)
    return factor_of


def deal_out(stream_key, own, number, rows, count, top, most, skew):
    sequence = jax.random.permutation(stream_key, count)
    packed, common = load_shares(count, rows * top, most, skew, True), load_shares(count, rows * top, most, skew, False)
    places = jnp.arange(count)

    def named(tallies, offset_by):
        used = int((tallies > 0).sum())
        fixed = max(1, used // 4)
        shifted = fixed + (places - fixed + offset_by * (used - fixed)) % max(1, count - fixed)
        return jnp.zeros((count,), jnp.int32).at[sequence[jnp.where(places < fixed, places, shifted)]].set(jnp.asarray(tallies, jnp.int32))

    tallies = jnp.where(number % 4 == 0, named(packed, number // 4), named(common, number - number // 4 - 1))
    mixed = jax.random.permutation(jax.random.fold_in(own, 3), count)
    source_of, sink = mixed[0:count // 2 * 2:2], mixed[1:count // 2 * 2:2]
    room = jnp.minimum(tallies[source_of] - 1, most - tallies[sink]) // 2
    room = jnp.where((source_of == sequence[0]) | (sink == sequence[0]) | (tallies[sink] == 0), 0, jnp.maximum(room, 0))
    shifted = jax.random.randint(jax.random.fold_in(own, 4), (count // 2,), 0, 1 << 20) % (room + 1)
    tallies = tallies.at[source_of].add(-shifted).at[sink].add(shifted)
    labels = jnp.searchsorted(jnp.cumsum(tallies), jnp.arange(rows * top), side="right").astype(jnp.int32)
    grid = labels.reshape(top, rows).T
    grid = grid[jax.random.permutation(jax.random.fold_in(own, 1), rows)]
    offset_by = jax.random.randint(jax.random.fold_in(own, 2), (rows, 1), 0, top)
    return jnp.take_along_axis(grid, (jnp.arange(top)[None, :] + offset_by) % top, axis=1)


def load_shares(number_of, total, bound, slope, full):
    loads = [(1 << 20) // math.isqrt(grade ** slope) + 1 for grade in range(1, number_of + 1)]
    largest = bound if full else min(bound, max(-(-total // number_of), total * loads[0] // sum(loads)))
    least = 1 if total - largest >= number_of - 1 else 0
    given, surplus = [largest] + [least] * (number_of - 1), total - largest - least * (number_of - 1)
    while surplus > 0:
        candidates = [i for i in range(1, number_of) if given[i] < largest] or [i for i in range(1, number_of) if given[i] < bound]
        pool, budget = sum([loads[i] for i in candidates]), surplus
        for i in candidates:
            extra = min(bound - given[i], max(1, budget * loads[i] // pool), surplus)
            given[i] = given[i] + extra
            surplus = surplus - extra
    return np.array(given)


def normal_values(stream_key, shape, scale, limit, cuts=(), kind=jnp.bfloat16):
    level = block_scale(stream_key, shape, cuts, -0.22, 0.18) if cuts else 1.0
    array = jax.random.normal(stream_key, shape, jnp.float32) * scale * level
    return jnp.minimum(jnp.maximum(array, -limit), limit).astype(kind)


def setup_inputs(seed: int = 0) -> dict:
    streams_of = jax.random.split(jax.random.key(seed), 9)
    tokens = normal_values(streams_of[0], (TOKENS, D), 1.0, 6.0, ((0, 128), (1, 8)))
    cotangent = normal_values(streams_of[1], (TOKENS, D), 1.0, 6.0, ((0, 128), (1, 8)))
    gate_logits = normal_values(streams_of[2], (TOKENS, PICKS), 1.5, 6.0, ((0, 128),), jnp.float32)
    node_groups_keys = jax.random.split(jax.random.fold_in(streams_of[3], 1), TOKENS // TOK_GROUP)
    node_groups_turns = jax.random.permutation(jax.random.fold_in(streams_of[3], 3), TOKENS // TOK_GROUP)
    node_groups = jax.vmap(lambda own, number: deal_out(jax.random.fold_in(streams_of[3], 2), own, number, TOK_GROUP, N_WIDE, PICKS, CAP, 2))(node_groups_keys, node_groups_turns).reshape((TOKENS, PICKS))
    sample_ids = with_ends(jax.random.randint(streams_of[4], (TOKENS,), 0, SAMPLES), jax.random.fold_in(streams_of[4], 1), 0, SAMPLES - 1).astype(jnp.int32)
    advantages = normal_values(streams_of[5], (SAMPLES,), 1.0, 4.0, (), jnp.float32)
    up_weight = normal_values(streams_of[6], (EXPERTS, D, FF), D ** -0.5, 0.09375, ((0, 128), (1, 8)))
    down_weight = normal_values(streams_of[7], (EXPERTS, FF, D), FF ** -0.5, 0.1875, ((0, 128), (2, 8)))
    return {"tokens": tokens, "cotangent": cotangent, "gate_logits": gate_logits, "node_groups": node_groups, "sample_ids": sample_ids, "advantages": advantages, "up_weight": up_weight, "down_weight": down_weight}


def silu_slope(pre):
    sig = jax.nn.sigmoid(pre)
    return sig * (1.0 + pre * (1.0 - sig))


def reference(tokens, cotangent, gate_logits, node_groups, sample_ids, advantages, up_weight, down_weight):
    tok_all, dim = tokens.shape
    picks = node_groups.shape[1]
    blocks = N_WIDE
    slots = CAP
    feat = dim // N_NARROW
    grouped = node_groups.reshape(blocks, TOK_GROUP * picks)
    onehot = (grouped[:, :, None] == jnp.arange(N_WIDE, dtype=jnp.int32)[None, None, :]).astype(jnp.int32)
    rank = jnp.sum((jnp.cumsum(onehot, axis=1) - onehot) * onehot, axis=2)
    route = jnp.arange(tok_all * picks, dtype=jnp.int32).reshape(blocks, TOK_GROUP * picks)
    block_id = jnp.arange(blocks, dtype=jnp.int32)[:, None]
    target = grouped * (blocks * slots) + block_id * slots + rank
    table = jnp.full((N_WIDE * blocks * slots,), tok_all * picks, jnp.int32)
    table = table.at[target.reshape(-1)].set(route.reshape(-1)).reshape(N_WIDE, blocks * slots)
    scores = jax.nn.sigmoid(gate_logits)
    total = jnp.sum(scores, axis=1, keepdims=True)
    weights = 2.5 * scores / total
    route_weights = jnp.concatenate([weights.reshape(-1), jnp.zeros((1,), jnp.float32)]).astype(jnp.bfloat16)
    tokens_pad = jnp.concatenate([tokens, jnp.zeros((1, dim), jnp.bfloat16)], axis=0)
    cot_pad = jnp.concatenate([cotangent, jnp.zeros((1, dim), jnp.bfloat16)], axis=0)
    rows = blocks * slots

    def step(carry, inputs):
        acc_out, acc_grad, acc_score = carry
        index, up, down = inputs
        token_index = index // picks
        rows_x = tokens_pad[token_index].reshape(rows, N_NARROW, feat).astype(jnp.float32)
        rows_c = cot_pad[token_index].reshape(rows, N_NARROW, feat).astype(jnp.float32)
        rows_w = route_weights[index].astype(jnp.float32)[:, None]
        up_blocks = up.reshape(N_NARROW, feat, FF).astype(jnp.float32)
        down_blocks = down.reshape(FF, N_NARROW, feat).astype(jnp.float32)
        up_part = jnp.einsum("rnd,ndf->rnf", rows_x, up_blocks).astype(jnp.bfloat16)
        back_part = jnp.einsum("rnd,fnd->rnf", rows_c, down_blocks).astype(jnp.bfloat16)
        up_part = lax.optimization_barrier(up_part)
        back_part = lax.optimization_barrier(back_part)
        pre = jnp.sum(up_part.astype(jnp.float32), axis=1)
        grad = jnp.sum(back_part.astype(jnp.float32), axis=1)
        hidden = jax.nn.silu(pre).astype(jnp.bfloat16)
        score = jnp.sum(hidden.astype(jnp.float32) * grad, axis=1).astype(jnp.bfloat16)
        hidden_grad = (rows_w * grad * silu_slope(pre)).astype(jnp.bfloat16)
        output = (rows_w * jnp.dot(hidden, down, preferred_element_type=jnp.float32)).astype(jnp.bfloat16)
        input_grad = jnp.dot(hidden_grad, up.T, preferred_element_type=jnp.float32).astype(jnp.bfloat16)
        acc_out = acc_out.at[token_index].add(output.astype(jnp.float32))
        acc_grad = acc_grad.at[token_index].add(input_grad.astype(jnp.float32))
        acc_score = acc_score.at[index].set(score)
        return (acc_out, acc_grad, acc_score), None

    start = (jnp.zeros((tok_all + 1, dim), jnp.float32), jnp.zeros((tok_all + 1, dim), jnp.float32),
             jnp.zeros((tok_all * picks + 1,), jnp.bfloat16))
    (acc_out, acc_grad, acc_score), _ = lax.scan(step, start, (table, up_weight, down_weight))
    mixed = acc_out[:tok_all].astype(jnp.bfloat16)
    advantage = advantages[sample_ids]
    token_grad = (advantage[:, None] * acc_grad[:tok_all]).astype(jnp.bfloat16)
    picked = acc_score[:tok_all * picks].astype(jnp.float32).reshape(tok_all, picks)
    mean_score = jnp.sum(weights * picked, axis=1, keepdims=True) / 2.5
    logit_grad = advantage[:, None] * (2.5 / total) * (picked - mean_score) * scores * (1.0 - scores)
    return mixed, token_grad, logit_grad
```

```python
import functools
import math

import jax
import jax.numpy as jnp
from jax import lax
from jax.experimental import pallas as pl
from jax.experimental.pallas import tpu as pltpu
from jax.sharding import PartitionSpec as P

MESH = pl.DeviceIdType.MESH
f32, bf16 = jnp.float32, jnp.bfloat16
SCALE = 2.5
CORES = 2
SLOTS = 2


def dot(a, b):
    return lax.dot_general(a, b, (((1,), (0,)), ((), ())), preferred_element_type=f32)


def dot_nt(a, b):
    return lax.dot_general(a, b, (((1,), (1,)), ((), ())), preferred_element_type=f32)


def dot_tn(a, b):
    return lax.dot_general(a, b, (((0,), (0,)), ((), ())), preferred_element_type=f32)


def rows_at(index, size):
    return pl.ds(pl.multiple_of(index * size, size), size)


def kernel(
    side, ring,
    tok_ref, cot_ref, gate_ref, group_ref, id_ref, adv_ref, up_hbm, down_hbm,
    mixed_ref, tgrad_ref, lgrad_ref,
    up_ref, down_ref, send, mid, mid2, land, part, inbox, both, outrow, score_box,
    w_sem, st_send, st_recv, ring_send, ring_recv, ag_send, ag_recv, tail_send, tail_recv,
):
    wide, me = lax.axis_index("wide"), lax.axis_index("narrow")
    my_y = lax.div(wide, side * CORES)
    my_z = lax.rem(lax.div(wide, CORES), side)
    my_c = lax.rem(wide, CORES)
    toks, feat = tok_ref.shape
    rows = send.shape[1]
    ff = up_ref.shape[1]
    big, small = rows // side, rows // (side * CORES)
    chunk = rows // ring
    half = ring // 2
    right, left = lax.rem(me + 1, ring), lax.rem(me + ring - 1, ring)

    def wide_of(y, z, c):
        return (y * side + z) * CORES + c

    def near(stream, k):
        if stream == 0:
            spot = lax.rem(my_z + k, side)
            return spot, wide_of(my_y, spot, my_c)
        spot = lax.rem(my_y + k, side)
        return spot, wide_of(spot, my_z, my_c)

    def far(stream, k):
        if stream == 0:
            spot = lax.rem(my_y * CORES + my_c + k, side * CORES)
            return spot, wide_of(lax.div(spot, CORES), my_z, lax.rem(spot, CORES))
        spot = lax.rem(my_z * CORES + my_c + k, side * CORES)
        return spot, wide_of(my_y, lax.div(spot, CORES), lax.rem(spot, CORES))

    my_near = (my_z, my_y)
    my_far = (my_y * CORES + my_c, my_z * CORES + my_c)

    barrier = pltpu.get_barrier_semaphore()

    def greet(target, narrow):
        pl.semaphore_signal(barrier, inc=1, device_id=(target, narrow), device_id_type=MESH)

    @pl.loop(1, side * CORES)
    def _(k):
        greet(far(1, k)[1], me)

    @pl.loop(1, side)
    def _(k):
        spot = lax.rem(my_y + k, side)
        greet(wide_of(spot, my_z, 0), me)
        greet(wide_of(spot, my_z, 1), me)

    @pl.loop(1, ring)
    def _(k):
        greet(wide, lax.rem(me + k, ring))

    greeted = side * CORES - 1 + (side - 1) * CORES + ring - 1

    up_copy = pltpu.make_async_copy(up_hbm.at[0], up_ref, w_sem.at[0])
    down_copy = pltpu.make_async_copy(down_hbm.at[0], down_ref, w_sem.at[1])
    up_copy.start()
    down_copy.start()

    groups = group_ref[...]
    gate = gate_ref[...]
    picks = groups.shape[1]
    scores = 1.0 / (1.0 + jnp.exp(-gate))
    total = jnp.sum(scores, axis=1, keepdims=True)
    weights = SCALE * scores / total
    lane = lax.broadcasted_iota(jnp.int32, (toks, rows), 1)
    pair = lane >> 1
    core, spot = pair & 1, pair >> 1
    slot = (lane & 1).astype(f32)
    first, second = spot // side, spot % side
    group_of = (wide_of(second, first, core), pair)
    earlier = (
        lax.broadcasted_iota(jnp.int32, (toks, toks), 1)
        < lax.broadcasted_iota(jnp.int32, (toks, toks), 0)
    ).astype(bf16)

    def route(stream):
        named = [groups[:, j : j + 1] == group_of[stream] for j in range(picks)]
        hit = functools.reduce(jnp.logical_or, named).astype(f32)
        rank = dot(earlier, hit.astype(bf16))
        mine = jnp.where(rank == slot, hit, 0.0)
        weighted = sum(jnp.where(named[j], weights[:, j : j + 1], 0.0) for j in range(picks))
        return mine, (mine * weighted).astype(bf16), named

    sources = (tok_ref, cot_ref)
    routes = [route(stream) for stream in range(2)]
    for stream in range(2):
        send[stream] = dot_tn(routes[stream][0].astype(bf16), sources[stream][...]).astype(bf16)

    def swap(forward):
        i = lax.broadcasted_iota(jnp.int32, (rows, rows), 0)
        j = lax.broadcasted_iota(jnp.int32, (rows, rows), 1)
        out, source = (i, j) if forward else (j, i)
        s, b, c, a = out & 1, (out >> 1) % side, (out >> 1) // side % CORES, (out >> 1) // (side * CORES)
        return (source == ((b * side + a) * CORES + c) * SLOTS + s).astype(bf16)

    def cross():
        i = lax.broadcasted_iota(jnp.int32, (rows, rows), 0)
        j = lax.broadcasted_iota(jnp.int32, (rows, rows), 1)
        s, b, c, a = i & 1, (i >> 1) % side, (i >> 1) // side % CORES, (i >> 1) // (side * CORES)
        return (j == ((b * CORES + c) * side + a) * SLOTS + s).astype(bf16)

    def remote(src, dst, s_sem, r_sem, target, narrow):
        return pltpu.make_async_remote_copy(
            src_ref=src, dst_ref=dst, send_sem=s_sem, recv_sem=r_sem,
            device_id=(target, narrow), device_id_type=MESH,
        )

    def near_stage(stage, stream, src, dst):
        mine = my_near[stream]

        @pl.loop(1, side)
        def _(k):
            spot, target = near(stream, k)
            remote(
                src.at[stream, rows_at(spot, big)], dst.at[stream, rows_at(mine, big)],
                st_send.at[stage, stream], st_recv.at[stage, stream], target, me,
            ).start()

        dst[stream, rows_at(mine, big)] = src[stream, rows_at(mine, big)]

    def far_stage(stage, stream, src, dst):
        mine = my_far[stream]

        @pl.loop(1, side * CORES)
        def _(k):
            spot, target = far(stream, k)
            remote(
                src.at[stream, rows_at(spot, small)], dst.at[stream, rows_at(mine, small)],
                st_send.at[stage, stream], st_recv.at[stage, stream], target, me,
            ).start()

        dst[stream, rows_at(mine, small)] = src[stream, rows_at(mine, small)]

    def landed(stage, stream, dst, part_of):
        view = dst.at[stream, pl.ds(0, rows - part_of)]
        pltpu.make_async_copy(view, view, st_recv.at[stage, stream]).wait()

    def gone(stage, stream, src, part_of):
        view = src.at[stream, pl.ds(0, rows - part_of)]
        pltpu.make_async_copy(view, view, st_send.at[stage, stream]).wait()

    pl.semaphore_wait(barrier, greeted)

    for stream in range(2):
        near_stage(0, stream, send, mid.at[0])
    for stream in range(2):
        landed(0, stream, mid.at[0], big)
        mid2[0, stream] = dot(swap(True), mid[0, stream]).astype(bf16)
        far_stage(1, stream, mid2.at[0], land)

    def ring_copy(kind, way, distance):
        owner = lax.rem(me + (distance if way == 0 else ring - distance), ring)
        return remote(
            part.at[kind, rows_at(owner, chunk)], inbox.at[kind, way, distance - 1],
            ring_send.at[kind, way, distance - 1], ring_recv.at[kind, way, distance - 1],
            wide, right if way == 0 else left,
        )

    def add_arrived(kind, way, distance):
        ring_copy(kind, way, distance).wait_recv()
        owner = lax.rem(me + (distance - 1 if way == 0 else ring - distance + 1), ring)
        spot = rows_at(owner, chunk)
        part[kind, spot] = (
            part[kind, spot].astype(f32) + inbox[kind, way, distance - 1].astype(f32)
        ).astype(bf16)

    def longest(kind, way):
        return half if kind == way else half - 1

    tile = min(256, ff)
    up_copy.wait()
    landed(1, 0, land, small)
    rows_x = land[0]

    @pl.loop(0, ff // tile)
    def _(n):
        cols = pl.ds(pl.multiple_of(n * tile, tile), tile)
        part[0, :, cols] = dot(rows_x, up_ref[:, cols]).astype(bf16)

    for way in (0, 1):
        if longest(0, way) > 0:
            ring_copy(0, way, longest(0, way)).start()
    down_copy.wait()
    landed(1, 1, land, small)
    rows_c = dot(cross(), land[1]).astype(bf16)

    @pl.loop(0, ff // tile)
    def _(n):
        cols = pl.ds(pl.multiple_of(n * tile, tile), tile)
        part[1, :, cols] = dot_nt(rows_c, down_ref[cols, :]).astype(bf16)

    for way in (1, 0):
        if longest(1, way) > 0:
            ring_copy(1, way, longest(1, way)).start()
    for later in range(half - 1):
        for kind, way in ((0, 0), (1, 1), (0, 1), (1, 0)):
            distance = longest(kind, way) - later
            if distance >= 2:
                add_arrived(kind, way, distance)
                ring_copy(kind, way, distance - 1).start()

    own = rows_at(me, chunk)
    sums = []
    for kind in (0, 1):
        acc = part[kind, own].astype(f32)
        for way in (0, 1):
            if longest(kind, way) > 0:
                ring_copy(kind, way, 1).wait_recv()
                acc = acc + inbox[kind, way, 0].astype(f32)
        sums.append(acc)
    pre, grad = sums
    sig = 1.0 / (1.0 + jnp.exp(-pre))
    both[0, own] = (pre * sig).astype(bf16)
    both[1, own] = (grad * (sig * (1.0 + pre * (1.0 - sig)))).astype(bf16)

    def pass_on(kind, way, distance):
        owner = lax.rem(me + (ring - distance + 1 if way == 0 else distance - 1), ring)
        view = both.at[kind, rows_at(owner, chunk)]
        return remote(
            view, view, ag_send.at[kind, way, distance - 1], ag_recv.at[kind, way, distance - 1],
            wide, right if way == 0 else left,
        )

    for kind in (0, 1):
        for way in (0, 1):
            if longest(kind, way) > 0:
                pass_on(kind, way, 1).start()
    for distance in range(1, half + 1):
        for kind, way in ((0, 0), (0, 1), (1, 0), (1, 1)):
            if distance <= longest(kind, way):
                pass_on(kind, way, distance).wait_recv()
                if distance < longest(kind, way):
                    pass_on(kind, way, distance + 1).start()

    wide_tile = min(256, feat)

    @pl.loop(0, feat // wide_tile)
    def _(n):
        cols = pl.ds(pl.multiple_of(n * wide_tile, wide_tile), wide_tile)
        outrow[0, 0, :, cols] = dot(both[0], down_ref[:, cols]).astype(bf16)

    far_stage(2, 0, outrow.at[0], mid.at[1])

    @pl.loop(0, feat // wide_tile)
    def _(n):
        cols = pl.ds(pl.multiple_of(n * wide_tile, wide_tile), wide_tile)
        mixed_rows = dot_nt(both[1], up_ref[cols, :]).astype(bf16)
        outrow[0, 1, :, cols] = dot(cross(), mixed_rows).astype(bf16)

    far_stage(2, 1, outrow.at[0], mid.at[1])
    for stream in range(2):
        landed(2, stream, mid.at[1], small)
        mid2[1, stream] = dot(swap(False), mid[1, stream]).astype(bf16)
        near_stage(3, stream, mid2.at[1], outrow.at[1])

    landed(3, 0, outrow.at[1], big)
    back = outrow[1, 0]
    mine, weighted, named = routes[0]
    products = dot_nt(cot_ref[...], back) * mine
    lane4 = lax.broadcasted_iota(jnp.int32, (toks, 128), 1)
    row4 = lax.broadcasted_iota(jnp.int32, (toks, 128), 0)
    packed = jnp.zeros((toks, 128), f32)
    for j in range(picks):
        column = jnp.sum(jnp.where(named[j], products, 0.0), axis=1, keepdims=True)
        packed = jnp.where(lane4 == row4 * picks + j, column, packed)
    score_box[rows_at(me, 8)] = jnp.broadcast_to(jnp.sum(packed, axis=0, keepdims=True), (8, 128))

    @pl.loop(1, ring)
    def _(k):
        view = score_box.at[rows_at(me, 8)]
        remote(view, view, tail_send, tail_recv, wide, lax.rem(me + k, ring)).start()

    mixed_ref[...] = dot(weighted, back).astype(bf16)
    ids = id_ref[...].astype(f32)
    square = lax.broadcasted_iota(jnp.int32, (toks, toks), 0) == lax.broadcasted_iota(
        jnp.int32, (toks, toks), 1
    )
    id_column = jnp.sum(jnp.where(square, ids, 0.0), axis=1, keepdims=True)
    samples = adv_ref.shape[1]
    match = id_column == lax.broadcasted_iota(jnp.int32, (toks, samples), 1).astype(f32)
    advantage = jnp.sum(jnp.where(match, adv_ref[...], 0.0), axis=1, keepdims=True)
    landed(3, 1, outrow.at[1], big)
    tgrad_ref[...] = (advantage * dot(routes[1][1], outrow[1, 1])).astype(bf16)

    tail_view = score_box.at[pl.ds(0, (ring - 1) * 8)]
    pltpu.make_async_copy(tail_view, tail_view, tail_recv).wait()
    summed = score_box[pl.ds(0, 8)]
    for other in range(1, ring):
        summed = summed + score_box[pl.ds(other * 8, 8)]
    spread = jnp.broadcast_to(summed[0:1], (toks, 128))
    lane_pick = lax.broadcasted_iota(jnp.int32, (toks, picks), 1)
    picked = jnp.zeros((toks, picks), f32)
    for j in range(picks):
        column = jnp.sum(jnp.where(lane4 == row4 * picks + j, spread, 0.0), axis=1, keepdims=True)
        picked = jnp.where(lane_pick == j, column, picked)
    mean_score = jnp.sum(weights * picked, axis=1, keepdims=True) / SCALE
    lgrad_ref[...] = (
        advantage * (SCALE / total) * (picked - mean_score) * scores * (1.0 - scores)
    )

    for stream in range(2):
        gone(0, stream, send, big)
        gone(1, stream, mid2.at[0], small)
        gone(2, stream, outrow.at[0], small)
        gone(3, stream, mid2.at[1], big)
    for kind in (0, 1):
        for way in (0, 1):
            for distance in range(1, longest(kind, way) + 1):
                ring_copy(kind, way, distance).wait_send()
                pass_on(kind, way, distance).wait_send()
    pltpu.make_async_copy(tail_view, tail_view, tail_send).wait()


def solution(mesh):
    ring = mesh.shape["narrow"]
    side = math.isqrt(mesh.shape["wide"] // CORES)

    def step(tokens, cotangent, gate, groups, ids, advantages, up, down):
        toks, feat = tokens.shape
        ff = up.shape[2]
        rows = mesh.shape["wide"] * SLOTS
        half = ring // 2
        vmem = pl.BlockSpec(memory_space=pltpu.VMEM)
        hbm = pl.BlockSpec(memory_space=pl.ANY)
        dma = pltpu.SemaphoreType.DMA
        return pl.pallas_call(
            functools.partial(kernel, side, ring),
            out_shape=(
                jax.ShapeDtypeStruct((toks, feat), bf16),
                jax.ShapeDtypeStruct((toks, feat), bf16),
                jax.ShapeDtypeStruct(gate.shape, f32),
            ),
            in_specs=[vmem] * 6 + [hbm] * 2,
            out_specs=[vmem] * 3,
            scratch_shapes=[
                pltpu.VMEM((feat, ff), bf16),
                pltpu.VMEM((ff, feat), bf16),
                pltpu.VMEM((2, rows, feat), bf16),
                pltpu.VMEM((2, 2, rows, feat), bf16),
                pltpu.VMEM((2, 2, rows, feat), bf16),
                pltpu.VMEM((2, rows, feat), bf16),
                pltpu.VMEM((2, rows, ff), bf16),
                pltpu.VMEM((2, 2, half, rows // ring, ff), bf16),
                pltpu.VMEM((2, rows, ff), bf16),
                pltpu.VMEM((2, 2, rows, feat), bf16),
                pltpu.VMEM((ring * 8, 128), f32),
                dma((2,)),
                dma((4, 2)),
                dma((4, 2)),
                dma((2, 2, half)),
                dma((2, 2, half)),
                dma((2, 2, half)),
                dma((2, 2, half)),
                dma,
                dma,
            ],
            compiler_params=pltpu.CompilerParams(
                collective_id=0, has_side_effects=True, vmem_limit_bytes=40 * 1024 * 1024
            ),
            cost_estimate=pl.CostEstimate(
                flops=8 * rows * feat * ff, bytes_accessed=4 * feat * ff, transcendentals=0
            ),
        )(
            tokens, cotangent, gate, groups, ids.reshape(1, toks), advantages.reshape(1, -1), up, down
        )

    in_specs = (
        P("wide", "narrow"),
        P("wide", "narrow"),
        P("wide", None),
        P("wide", None),
        P("wide"),
        P(),
        P("wide", "narrow", None),
        P("wide", None, "narrow"),
    )
    out_specs = (P("wide", "narrow"), P("wide", "narrow"), P("wide", None))
    return jax.shard_map(step, mesh=mesh, in_specs=in_specs, out_specs=out_specs, check_vma=False)
```

```python
import functools
import math

import jax
import jax.numpy as jnp
from jax import lax
from jax.experimental import pallas as pl
from jax.experimental.pallas import tpu as pltpu
from jax.sharding import PartitionSpec as P

MESH = pl.DeviceIdType.MESH
f32, bf16 = jnp.float32, jnp.bfloat16
SCALE = 2.5
CORES = 2
SLOTS = 2


def dot(a, b):
    return lax.dot_general(a, b, (((1,), (0,)), ((), ())), preferred_element_type=f32)


def dot_nt(a, b):
    return lax.dot_general(a, b, (((1,), (1,)), ((), ())), preferred_element_type=f32)


def dot_tn(a, b):
    return lax.dot_general(a, b, (((0,), (0,)), ((), ())), preferred_element_type=f32)


def rows_at(index, size):
    return pl.ds(pl.multiple_of(index * size, size), size)


def kernel(
    side, ring,
    tok_hbm, cot_hbm, gate_hbm, group_hbm, id_hbm, adv_hbm, up_hbm, down_hbm,
    mixed_ref, tgrad_ref, lgrad_ref,
    tok_ref, cot_ref, gate_ref, group_ref, id_ref, adv_ref, up_ref, down_ref,
    send, mid, mid2, land, part, inbox, both, outrow, score_box,
    w_sem, st_send, st_recv, ring_send, ring_recv, ag_send, ag_recv, tail_send, tail_recv,
):
    wide, me = lax.axis_index("wide"), lax.axis_index("narrow")
    my_y = lax.div(wide, side * CORES)
    my_z = lax.rem(lax.div(wide, CORES), side)
    my_c = lax.rem(wide, CORES)
    toks, feat = tok_ref.shape
    rows = send.shape[1]
    ff = up_ref.shape[1]
    big, small = rows // side, rows // (side * CORES)
    chunk = rows // ring
    half = ring // 2
    right, left = lax.rem(me + 1, ring), lax.rem(me + ring - 1, ring)

    def wide_of(y, z, c):
        return (y * side + z) * CORES + c

    def near(stream, k):
        if stream == 0:
            spot = lax.rem(my_z + k, side)
            return spot, wide_of(my_y, spot, my_c)
        spot = lax.rem(my_y + k, side)
        return spot, wide_of(spot, my_z, my_c)

    def far(stream, k):
        if stream == 0:
            spot = lax.rem(my_y * CORES + my_c + k, side * CORES)
            return spot, wide_of(lax.div(spot, CORES), my_z, lax.rem(spot, CORES))
        spot = lax.rem(my_z * CORES + my_c + k, side * CORES)
        return spot, wide_of(my_y, lax.div(spot, CORES), lax.rem(spot, CORES))

    my_near = (my_z, my_y)
    my_far = (my_y * CORES + my_c, my_z * CORES + my_c)

    loads = [
        pltpu.make_async_copy(source, target, w_sem.at[i])
        for i, (source, target) in enumerate((
            (group_hbm, group_ref), (gate_hbm, gate_ref), (tok_hbm, tok_ref), (cot_hbm, cot_ref),
            (id_hbm, id_ref), (adv_hbm, adv_ref), (up_hbm.at[0], up_ref), (down_hbm.at[0], down_ref),
        ))
    ]
    up_copy, down_copy = loads[6:]
    for load in loads:
        load.start()

    barrier = pltpu.get_barrier_semaphore()

    def greet(target, narrow):
        pl.semaphore_signal(barrier, inc=1, device_id=(target, narrow), device_id_type=MESH)

    @pl.loop(1, side * CORES)
    def _(k):
        greet(far(1, k)[1], me)

    @pl.loop(1, side)
    def _(k):
        spot = lax.rem(my_y + k, side)
        greet(wide_of(spot, my_z, 0), me)
        greet(wide_of(spot, my_z, 1), me)

    @pl.loop(1, ring)
    def _(k):
        greet(wide, lax.rem(me + k, ring))

    greeted = side * CORES - 1 + (side - 1) * CORES + ring - 1

    for load in loads[:6]:
        load.wait()

    picks = group_ref.shape[0]
    scores = 1.0 / (1.0 + jnp.exp(-gate_ref[...]))
    total = jnp.sum(scores, axis=0, keepdims=True)
    weights = SCALE * scores / total
    square = lax.broadcasted_iota(jnp.int32, (toks, toks), 0) == lax.broadcasted_iota(
        jnp.int32, (toks, toks), 1
    )

    def column(row):
        return jnp.sum(jnp.where(square, row, 0.0), axis=1, keepdims=True)

    groups = [column(group_ref[j : j + 1].astype(f32)).astype(jnp.int32) for j in range(picks)]
    weight = [column(weights[j : j + 1]) for j in range(picks)]
    lane = lax.broadcasted_iota(jnp.int32, (toks, rows), 1)
    pair = lane >> 1
    core, spot = pair & 1, pair >> 1
    slot = (lane & 1).astype(f32)
    first, second = spot // side, spot % side
    group_of = (wide_of(second, first, core), pair)
    earlier = (
        lax.broadcasted_iota(jnp.int32, (toks, toks), 1)
        < lax.broadcasted_iota(jnp.int32, (toks, toks), 0)
    ).astype(bf16)

    def route(stream):
        named = [groups[j] == group_of[stream] for j in range(picks)]
        hit = functools.reduce(jnp.logical_or, named).astype(f32)
        rank = dot(earlier, hit.astype(bf16))
        mine = jnp.where(rank == slot, hit, 0.0)
        weighted = sum(jnp.where(named[j], weight[j], 0.0) for j in range(picks))
        return mine, (mine * weighted).astype(bf16), named

    sources = (tok_ref, cot_ref)
    routes = [route(stream) for stream in range(2)]
    for stream in range(2):
        send[stream] = dot_tn(routes[stream][0].astype(bf16), sources[stream][...]).astype(bf16)

    def swap(forward):
        i = lax.broadcasted_iota(jnp.int32, (rows, rows), 0)
        j = lax.broadcasted_iota(jnp.int32, (rows, rows), 1)
        out, source = (i, j) if forward else (j, i)
        s, b, c, a = out & 1, (out >> 1) % side, (out >> 1) // side % CORES, (out >> 1) // (side * CORES)
        return (source == ((b * side + a) * CORES + c) * SLOTS + s).astype(bf16)

    def cross():
        i = lax.broadcasted_iota(jnp.int32, (rows, rows), 0)
        j = lax.broadcasted_iota(jnp.int32, (rows, rows), 1)
        s, b, c, a = i & 1, (i >> 1) % side, (i >> 1) // side % CORES, (i >> 1) // (side * CORES)
        return (j == ((b * CORES + c) * side + a) * SLOTS + s).astype(bf16)

    def remote(src, dst, s_sem, r_sem, target, narrow):
        return pltpu.make_async_remote_copy(
            src_ref=src, dst_ref=dst, send_sem=s_sem, recv_sem=r_sem,
            device_id=(target, narrow), device_id_type=MESH,
        )

    def near_stage(stage, stream, src, dst):
        mine = my_near[stream]

        @pl.loop(1, side)
        def _(k):
            spot, target = near(stream, k)
            remote(
                src.at[stream, rows_at(spot, big)], dst.at[stream, rows_at(mine, big)],
                st_send.at[stage, stream], st_recv.at[stage, stream], target, me,
            ).start()

        dst[stream, rows_at(mine, big)] = src[stream, rows_at(mine, big)]

    def far_stage(stage, stream, src, dst):
        mine = my_far[stream]

        @pl.loop(1, side * CORES)
        def _(k):
            spot, target = far(stream, k)
            remote(
                src.at[stream, rows_at(spot, small)], dst.at[stream, rows_at(mine, small)],
                st_send.at[stage, stream], st_recv.at[stage, stream], target, me,
            ).start()

        dst[stream, rows_at(mine, small)] = src[stream, rows_at(mine, small)]

    def landed(stage, stream, dst, part_of):
        view = dst.at[stream, pl.ds(0, rows - part_of)]
        pltpu.make_async_copy(view, view, st_recv.at[stage, stream]).wait()

    def gone(stage, stream, src, part_of):
        view = src.at[stream, pl.ds(0, rows - part_of)]
        pltpu.make_async_copy(view, view, st_send.at[stage, stream]).wait()

    pl.semaphore_wait(barrier, greeted)

    for stream in range(2):
        near_stage(0, stream, send, mid.at[0])
    for stream in range(2):
        landed(0, stream, mid.at[0], big)
        mid2[0, stream] = dot(swap(True), mid[0, stream]).astype(bf16)
        far_stage(1, stream, mid2.at[0], land)

    def nearer(distance):
        return half - 2 if distance == half >= 3 else distance - 1

    def longest(kind, way):
        return half if kind == way else half - 1

    def beside(way, hops):
        return lax.rem(me + (hops if way == 0 else ring - hops), ring)

    def ring_copy(kind, way, distance):
        owner = beside(way, distance)
        return remote(
            part.at[kind, rows_at(owner, chunk)], inbox.at[kind, way, distance - 1],
            ring_send.at[kind, way, distance - 1], ring_recv.at[kind, way, distance - 1],
            wide, beside(way, distance - nearer(distance)),
        )

    def add_arrived(kind, way, place):
        spot = rows_at(beside(way, place), chunk)
        acc = part[kind, spot].astype(f32)
        for distance in range(1, longest(kind, way) + 1):
            if nearer(distance) == place:
                ring_copy(kind, way, distance).wait_recv()
                acc = acc + inbox[kind, way, distance - 1].astype(f32)
        part[kind, spot] = acc.astype(bf16)

    def set_off(kind, way):
        for distance in range(longest(kind, way), 0, -1):
            if not any(nearer(d) == distance for d in range(1, longest(kind, way) + 1)):
                ring_copy(kind, way, distance).start()

    tile = min(256, ff)
    up_copy.wait()
    landed(1, 0, land, small)
    rows_x = land[0]

    @pl.loop(0, ff // tile)
    def _(n):
        cols = pl.ds(pl.multiple_of(n * tile, tile), tile)
        part[0, :, cols] = dot(rows_x, up_ref[:, cols]).astype(bf16)

    set_off(0, 0)
    set_off(0, 1)
    down_copy.wait()
    landed(1, 1, land, small)
    rows_c = dot(cross(), land[1]).astype(bf16)

    @pl.loop(0, ff // tile)
    def _(n):
        cols = pl.ds(pl.multiple_of(n * tile, tile), tile)
        part[1, :, cols] = dot_nt(rows_c, down_ref[cols, :]).astype(bf16)

    set_off(1, 1)
    set_off(1, 0)
    for place in range(half - 1, 0, -1):
        for kind, way in ((0, 0), (0, 1), (1, 1), (1, 0)):
            if any(nearer(d) == place for d in range(1, longest(kind, way) + 1)):
                add_arrived(kind, way, place)
                ring_copy(kind, way, place).start()

    own = rows_at(me, chunk)

    def summed_here(kind):
        acc = part[kind, own].astype(f32)
        for way in (0, 1):
            for distance in range(1, longest(kind, way) + 1):
                if nearer(distance) == 0:
                    ring_copy(kind, way, distance).wait_recv()
                    acc = acc + inbox[kind, way, distance - 1].astype(f32)
        return acc

    def pass_on(kind, way, distance):
        held = nearer(distance)
        view = both.at[kind, rows_at(beside(1 - way, held), chunk)]
        return remote(
            view, view, ag_send.at[kind, way, distance - 1], ag_recv.at[kind, way, distance - 1],
            wide, beside(way, distance - held),
        )

    def hand_on(kind, way, held):
        for distance in range(1, longest(kind, way) + 1):
            if nearer(distance) == held:
                pass_on(kind, way, distance).start()

    def product(kind, owners):
        spots = [rows_at(owner, chunk) for owner in owners]
        block = jnp.concatenate([both[kind, spot] for spot in spots], axis=0)
        out = dot(block, down_ref[...]) if kind == 0 else dot_nt(block, up_ref[...])
        out = out.astype(bf16)
        for i, (owner, spot) in enumerate(zip(owners, spots)):
            outrow[0, kind, spot] = out[i * chunk : (i + 1) * chunk]
            if kind == 0:
                for core_to in range(CORES):
                    goal = owner * CORES + core_to
                    at_home = goal == my_far[0]

                    @pl.when(at_home)
                    def _():
                        mid[1, 0, rows_at(goal, small)] = out[
                            i * chunk + core_to * small : i * chunk + (core_to + 1) * small
                        ]

                    @pl.when(jnp.logical_not(at_home))
                    def _():
                        remote(
                            outrow.at[0, 0, rows_at(goal, small)],
                            mid.at[1, 0, rows_at(my_far[0], small)],
                            st_send.at[2, 0], st_recv.at[2, 0], wide_of(owner, my_z, core_to), me,
                        ).start()

    pre = summed_here(0)
    sig = 1.0 / (1.0 + jnp.exp(-pre))
    both[0, own] = (pre * sig).astype(bf16)
    for way in (0, 1):
        hand_on(0, way, 0)
    slope = sig * (1.0 + pre * (1.0 - sig))
    both[1, own] = (summed_here(1) * slope).astype(bf16)
    for way in (1, 0):
        hand_on(1, way, 0)
    for kind in (0, 1):
        product(kind, [me])
    steps = sorted({nearer(d) for d in range(1, half + 1)})
    for held in steps:
        for kind in (0, 1):
            for way in (0, 1):
                for distance in range(1, longest(kind, way) + 1):
                    if nearer(distance) == held:
                        pass_on(kind, way, distance).wait_recv()
                        hand_on(kind, way, distance)
        for kind in (0, 1):
            product(kind, [
                beside(1 - way, distance)
                for way in (0, 1)
                for distance in range(1, longest(kind, way) + 1)
                if nearer(distance) == held
            ])

    wide_tile = min(256, feat)

    @pl.loop(0, feat // wide_tile)
    def _(n):
        cols = pl.ds(pl.multiple_of(n * wide_tile, wide_tile), wide_tile)
        outrow[2, 1, :, cols] = dot(cross(), outrow[0, 1, :, cols]).astype(bf16)

    far_stage(2, 1, outrow.at[2], mid.at[1])
    for stream in range(2):
        landed(2, stream, mid.at[1], small)
        mid2[1, stream] = dot(swap(False), mid[1, stream]).astype(bf16)
        near_stage(3, stream, mid2.at[1], outrow.at[1])

    landed(3, 0, outrow.at[1], big)
    back = outrow[1, 0]
    mine, weighted, named = routes[0]
    products = dot_nt(cot_ref[...], back) * mine
    lane_of = lax.broadcasted_iota(jnp.int32, (toks, 128), 1)
    row_of = lax.broadcasted_iota(jnp.int32, (toks, 128), 0)
    pick_of = lax.broadcasted_iota(jnp.int32, (8, 128), 0)
    packed = jnp.zeros((8, 128), f32)
    for j in range(picks):
        score = jnp.sum(jnp.where(named[j], products, 0.0), axis=1, keepdims=True)
        score = jnp.sum(jnp.where(lane_of == row_of, score, 0.0), axis=0, keepdims=True)
        packed = jnp.where(pick_of == j, score, packed)
    score_box[rows_at(me, 8)] = packed

    @pl.loop(1, ring)
    def _(k):
        view = score_box.at[rows_at(me, 8)]
        remote(view, view, tail_send, tail_recv, wide, lax.rem(me + k, ring)).start()

    mixed_ref[...] = dot(weighted, back).astype(bf16)
    id_column = column(id_ref[...].astype(f32))
    samples = adv_ref.shape[1]
    match = id_column == lax.broadcasted_iota(jnp.int32, (toks, samples), 1).astype(f32)
    advantage = jnp.sum(jnp.where(match, adv_ref[...], 0.0), axis=1, keepdims=True)
    landed(3, 1, outrow.at[1], big)
    tgrad_ref[...] = (advantage * dot(routes[1][1], outrow[1, 1])).astype(bf16)

    tail_view = score_box.at[pl.ds(0, (ring - 1) * 8)]
    pltpu.make_async_copy(tail_view, tail_view, tail_recv).wait()
    summed = score_box[pl.ds(0, 8)]
    for other in range(1, ring):
        summed = summed + score_box[pl.ds(other * 8, 8)]
    picked = summed[:picks, :toks]
    mean_score = jnp.sum(weights * picked, axis=0, keepdims=True) / SCALE
    row_advantage = jnp.sum(jnp.where(square, advantage, 0.0), axis=0, keepdims=True)
    lgrad_ref[...] = (
        row_advantage * (SCALE / total) * (picked - mean_score) * scores * (1.0 - scores)
    )

    for stream in range(2):
        gone(0, stream, send, big)
        gone(1, stream, mid2.at[0], small)
        gone(2, stream, outrow.at[2 * stream], small)
        gone(3, stream, mid2.at[1], big)
    for kind in (0, 1):
        for way in (0, 1):
            for distance in range(1, longest(kind, way) + 1):
                ring_copy(kind, way, distance).wait_send()
                pass_on(kind, way, distance).wait_send()
    pltpu.make_async_copy(tail_view, tail_view, tail_send).wait()


def solution(mesh):
    ring = mesh.shape["narrow"]
    side = math.isqrt(mesh.shape["wide"] // CORES)

    def step(tokens, cotangent, gate, groups, ids, advantages, up, down):
        toks, feat = tokens.shape
        ff = up.shape[2]
        rows = mesh.shape["wide"] * SLOTS
        half = ring // 2
        vmem = pl.BlockSpec(memory_space=pltpu.VMEM)
        hbm = pl.BlockSpec(memory_space=pltpu.HBM)
        dma = pltpu.SemaphoreType.DMA
        mixed, token_grad, logit_grad = pl.pallas_call(
            functools.partial(kernel, side, ring),
            out_shape=(
                jax.ShapeDtypeStruct((toks, feat), bf16),
                jax.ShapeDtypeStruct((toks, feat), bf16),
                jax.ShapeDtypeStruct(gate.shape[::-1], f32),
            ),
            in_specs=[hbm] * 8,
            out_specs=[vmem] * 3,
            scratch_shapes=[
                pltpu.VMEM((toks, feat), bf16),
                pltpu.VMEM((toks, feat), bf16),
                pltpu.VMEM(gate.shape[::-1], f32),
                pltpu.VMEM(gate.shape[::-1], jnp.int32),
                pltpu.VMEM((1, toks), jnp.int32),
                pltpu.VMEM((1, advantages.shape[0]), f32),
                pltpu.VMEM((feat, ff), bf16),
                pltpu.VMEM((ff, feat), bf16),
                pltpu.VMEM((2, rows, feat), bf16),
                pltpu.VMEM((2, 2, rows, feat), bf16),
                pltpu.VMEM((2, 2, rows, feat), bf16),
                pltpu.VMEM((2, rows, feat), bf16),
                pltpu.VMEM((2, rows, ff), bf16),
                pltpu.VMEM((2, 2, half, rows // ring, ff), bf16),
                pltpu.VMEM((2, rows, ff), bf16),
                pltpu.VMEM((3, 2, rows, feat), bf16),
                pltpu.VMEM((ring * 8, 128), f32),
                dma((8,)),
                dma((4, 2)),
                dma((4, 2)),
                dma((2, 2, half)),
                dma((2, 2, half)),
                dma((2, 2, half)),
                dma((2, 2, half)),
                dma,
                dma,
            ],
            compiler_params=pltpu.CompilerParams(
                collective_id=0, has_side_effects=True, vmem_limit_bytes=62 * 1024 * 1024
            ),
            cost_estimate=pl.CostEstimate(
                flops=8 * rows * feat * ff, bytes_accessed=4 * feat * ff, transcendentals=0
            ),
        )(
            tokens, cotangent, gate.T, groups.T, ids.reshape(1, toks), advantages.reshape(1, -1), up, down
        )
        return mixed, token_grad, logit_grad.T

    in_specs = (
        P("wide", "narrow"),
        P("wide", "narrow"),
        P("wide", None),
        P("wide", None),
        P("wide"),
        P(),
        P("wide", "narrow", None),
        P("wide", None, "narrow"),
    )
    out_specs = (P("wide", "narrow"), P("wide", "narrow"), P("wide", None))
    return jax.shard_map(step, mesh=mesh, in_specs=in_specs, out_specs=out_specs, check_vma=False)
```

```python
import functools
import math

import jax
import jax.numpy as jnp
from jax import lax
from jax.experimental import pallas as pl
from jax.experimental.pallas import tpu as pltpu
from jax.sharding import PartitionSpec as P

MESH = pl.DeviceIdType.MESH
f32, bf16 = jnp.float32, jnp.bfloat16
SCALE = 2.5
CORES = 2
SLOTS = 2
SIDE_COLS = 128


def dot(a, b):
    return lax.dot_general(a, b, (((1,), (0,)), ((), ())), preferred_element_type=f32)


def dot_nt(a, b):
    return lax.dot_general(a, b, (((1,), (1,)), ((), ())), preferred_element_type=f32)


def dot_tn(a, b):
    return lax.dot_general(a, b, (((0,), (0,)), ((), ())), preferred_element_type=f32)


def rows_at(index, size):
    return pl.ds(pl.multiple_of(index * size, size), size)


def kernel(
    side, ring,
    tok_hbm, cot_hbm, gate_hbm, group_hbm, id_hbm, adv_hbm, up_hbm, down_hbm,
    mixed_ref, tgrad_ref, lgrad_ref,
    tok_ref, cot_ref, gate_ref, group_ref, id_ref, adv_ref, up_ref, down_ref,
    send_x, send_c, mid_x, mid_c, turn_x, turn_c, land_x, land_c, crossed, part, inbox, hidden, slopes,
    out_y, out_g, leave_g, back_y, back_g, back_turn_y, back_turn_g, home_y, home_g, orders,
    w_sem, st_send, st_recv, ring_send, ring_recv, ag_send, ag_recv,
):
    wide, me = lax.axis_index("wide"), lax.axis_index("narrow")
    my_y = lax.div(wide, side * CORES)
    my_z = lax.rem(lax.div(wide, CORES), side)
    my_c = lax.rem(wide, CORES)
    toks, feat = tok_ref.shape
    rows = send_x.shape[0]
    ff = up_ref.shape[1]
    big, small = rows // side, rows // (side * CORES)
    chunk = rows // ring
    half = ring // 2
    all_cols = pl.ds(0, feat + SIDE_COLS)
    halves = [pl.ds(i * (feat // 2), feat // 2) for i in range(2)]
    def nearer(distance):
        return half - 2 if distance == half >= 3 else distance - 1

    hops = {distance - nearer(distance) for distance in range(1, half + 1)}

    def wide_of(y, z, c):
        return (y * side + z) * CORES + c

    def near(stream, k):
        if stream == 0:
            spot = lax.rem(my_z + k, side)
            return spot, wide_of(my_y, spot, my_c)
        spot = lax.rem(my_y + k, side)
        return spot, wide_of(spot, my_z, my_c)

    def far(stream, k):
        if stream == 0:
            spot = lax.rem(my_y * CORES + my_c + k, side * CORES)
            return spot, wide_of(lax.div(spot, CORES), my_z, lax.rem(spot, CORES))
        spot = lax.rem(my_z * CORES + my_c + k, side * CORES)
        return spot, wide_of(my_y, lax.div(spot, CORES), lax.rem(spot, CORES))

    my_near = (my_z, my_y)
    my_far = (my_y * CORES + my_c, my_z * CORES + my_c)

    loads = [
        pltpu.make_async_copy(source, target, w_sem.at[i])
        for i, (source, target) in enumerate((
            (group_hbm, group_ref), (gate_hbm, gate_ref), (tok_hbm, tok_ref), (cot_hbm, cot_ref),
            (id_hbm, id_ref), (adv_hbm, adv_ref), (up_hbm.at[0], up_ref), (down_hbm.at[0], down_ref),
        ))
    ]
    up_copy, down_copy = loads[6:]
    for load in loads:
        load.start()

    barrier = pltpu.get_barrier_semaphore()

    def greet(target, narrow):
        pl.semaphore_signal(barrier, inc=1, device_id=(target, narrow), device_id_type=MESH)

    @pl.loop(1, side * CORES)
    def _(k):
        greet(far(1, k)[1], me)

    @pl.loop(1, side)
    def _(k):
        spot = lax.rem(my_y + k, side)
        greet(wide_of(spot, my_z, 0), me)
        greet(wide_of(spot, my_z, 1), me)

    offsets = sorted({hop for hop in hops} | {ring - hop for hop in hops})
    for offset in offsets:
        greet(wide, lax.rem(me + offset, ring))

    greeted = side * CORES - 1 + (side - 1) * CORES + len(offsets)

    for load in loads[:6]:
        load.wait()

    picks = group_ref.shape[0]
    scores = 1.0 / (1.0 + jnp.exp(-gate_ref[...]))
    total = jnp.sum(scores, axis=0, keepdims=True)
    weights = SCALE * scores / total
    square = lax.broadcasted_iota(jnp.int32, (toks, toks), 0) == lax.broadcasted_iota(
        jnp.int32, (toks, toks), 1
    )

    def column(row):
        return jnp.sum(jnp.where(square, row, 0.0), axis=1, keepdims=True)

    groups = [column(group_ref[j : j + 1].astype(f32)).astype(jnp.int32) for j in range(picks)]
    weight = [column(weights[j : j + 1]) for j in range(picks)]
    lane = lax.broadcasted_iota(jnp.int32, (toks, rows), 1)
    pair = lane >> 1
    core, spot = pair & 1, pair >> 1
    slot = (lane & 1).astype(f32)
    first, second = spot // side, spot % side
    group_of = (wide_of(second, first, core), pair)
    earlier = (
        lax.broadcasted_iota(jnp.int32, (toks, toks), 1)
        < lax.broadcasted_iota(jnp.int32, (toks, toks), 0)
    ).astype(bf16)

    def route(stream):
        named = [groups[j] == group_of[stream] for j in range(picks)]
        hit = functools.reduce(jnp.logical_or, named).astype(f32)
        rank = dot(earlier, hit.astype(bf16))
        mine = jnp.where(rank == slot, hit, 0.0)
        weighted = sum(jnp.where(named[j], weight[j], 0.0) for j in range(picks))
        return mine, (mine * weighted).astype(bf16), named

    sources = (tok_ref, cot_ref)
    routes = []

    def pack(stream):
        routes.append(route(stream))
        sends[stream][...] = dot_tn(routes[stream][0].astype(bf16), sources[stream][...]).astype(bf16)

    def swap(forward):
        i = lax.broadcasted_iota(jnp.int32, (rows, rows), 0)
        j = lax.broadcasted_iota(jnp.int32, (rows, rows), 1)
        out, source = (i, j) if forward else (j, i)
        s, b, c, a = out & 1, (out >> 1) % side, (out >> 1) // side % CORES, (out >> 1) // (side * CORES)
        return (source == ((b * side + a) * CORES + c) * SLOTS + s).astype(bf16)

    def cross():
        i = lax.broadcasted_iota(jnp.int32, (rows, rows), 0)
        j = lax.broadcasted_iota(jnp.int32, (rows, rows), 1)
        s, b, c, a = i & 1, (i >> 1) % side, (i >> 1) // side % CORES, (i >> 1) // (side * CORES)
        return (j == ((b * CORES + c) * side + a) * SLOTS + s).astype(bf16)

    def remote(src, dst, s_sem, r_sem, target, narrow):
        return pltpu.make_async_remote_copy(
            src_ref=src, dst_ref=dst, send_sem=s_sem, recv_sem=r_sem,
            device_id=(target, narrow), device_id_type=MESH,
        )

    def near_stage(stage, stream, half_of, src, dst, cols):
        mine = my_near[stream]

        @pl.loop(1, side)
        def _(k):
            spot, target = near(stream, k)
            remote(
                src.at[rows_at(spot, big), cols], dst.at[rows_at(mine, big), cols],
                st_send.at[stage, stream, half_of], st_recv.at[stage, stream, half_of], target, me,
            ).start()

        dst[rows_at(mine, big), cols] = src[rows_at(mine, big), cols]

    def far_stage(stage, stream, half_of, src, dst, cols):
        mine = my_far[stream]

        @pl.loop(1, side * CORES)
        def _(k):
            spot, target = far(stream, k)
            remote(
                src.at[rows_at(spot, small), cols], dst.at[rows_at(mine, small), cols],
                st_send.at[stage, stream, half_of], st_recv.at[stage, stream, half_of], target, me,
            ).start()

        dst[rows_at(mine, small), cols] = src[rows_at(mine, small), cols]

    def landed(stage, stream, half_of, dst, part_of, cols):
        view = dst.at[pl.ds(0, rows - part_of), cols]
        pltpu.make_async_copy(view, view, st_recv.at[stage, stream, half_of]).wait()

    def gone(stage, stream, half_of, src, part_of, cols):
        view = src.at[pl.ds(0, rows - part_of), cols]
        pltpu.make_async_copy(view, view, st_send.at[stage, stream, half_of]).wait()

    sends, mids, turns, lands = (send_x, send_c), (mid_x, mid_c), (turn_x, turn_c), (land_x, land_c)
    pack(0)
    pl.semaphore_wait(barrier, greeted)
    for stream in range(2):
        if stream == 1:
            pack(1)
        for h, cols in enumerate(halves):
            near_stage(0, stream, h, sends[stream], mids[stream], cols)
    orders[0] = swap(True)
    orders[1] = cross()
    orders[2] = swap(False)
    id_column = column(id_ref[...].astype(f32))
    samples = adv_ref.shape[1]
    match = id_column == lax.broadcasted_iota(jnp.int32, (toks, samples), 1).astype(f32)
    advantage = jnp.sum(jnp.where(match, adv_ref[...], 0.0), axis=1, keepdims=True)
    row_advantage = jnp.sum(jnp.where(square, advantage, 0.0), axis=0, keepdims=True)
    for h, cols in enumerate(halves):
        for stream in range(2):
            landed(0, stream, h, mids[stream], big, cols)
            turns[stream][:, cols] = dot(orders[0], mids[stream][:, cols]).astype(bf16)
            far_stage(1, stream, h, turns[stream], lands[stream], cols)

    def longest(kind, way):
        return half if kind == way else half - 1

    def beside(way, hops):
        return lax.rem(me + (hops if way == 0 else ring - hops), ring)

    def ring_copy(kind, way, distance):
        owner = beside(way, distance)
        return remote(
            part.at[kind, rows_at(owner, chunk)], inbox.at[kind, way, distance - 1],
            ring_send.at[kind, way, distance - 1], ring_recv.at[kind, way, distance - 1],
            wide, beside(way, distance - nearer(distance)),
        )

    def add_arrived(kind, way, place):
        spot = rows_at(beside(way, place), chunk)
        acc = part[kind, spot].astype(f32)
        for distance in range(1, longest(kind, way) + 1):
            if nearer(distance) == place:
                ring_copy(kind, way, distance).wait_recv()
                acc = acc + inbox[kind, way, distance - 1].astype(f32)
        part[kind, spot] = acc.astype(bf16)

    def starts(kind, way):
        reach = range(1, longest(kind, way) + 1)
        return [d for d in reach if not any(nearer(other) == d for other in reach)]

    def set_off(kind):
        for way in (0, 1):
            for distance in starts(kind, way):
                ring_copy(kind, way, distance).start()

    tile = min(256, ff)
    early = sorted({
        (distance if way == 0 else ring - distance) % ring
        for kind in (0, 1) for way in (0, 1) for distance in starts(kind, way)
    })
    late = [offset for offset in range(ring) if offset not in early]

    def partial(kind, offsets_of):
        spots = [rows_at(lax.rem(me + offset, ring), chunk) for offset in offsets_of]
        source = crossed if kind else land_x
        block = jnp.concatenate([source[spot] for spot in spots], axis=0)

        @pl.loop(0, ff // tile)
        def _(n):
            cols = pl.ds(pl.multiple_of(n * tile, tile), tile)
            out = dot_nt(block, down_ref[cols, :]) if kind else dot(block, up_ref[:, cols])
            out = out.astype(bf16)
            for i, spot in enumerate(spots):
                part[kind, spot, cols] = out[i * chunk : (i + 1) * chunk]

    up_copy.wait()
    for h, cols in enumerate(halves):
        landed(1, 0, h, land_x, small, cols)
    partial(0, early)
    set_off(0)
    down_copy.wait()
    for h, cols in enumerate(halves):
        landed(1, 1, h, land_c, small, cols)
    crossed[...] = dot(orders[1], land_c[...]).astype(bf16)
    partial(1, early)
    set_off(1)
    if late:
        partial(0, late)
        partial(1, late)
    for place in range(half - 1, 0, -1):
        for kind, way in ((0, 0), (0, 1), (1, 1), (1, 0)):
            if any(nearer(d) == place for d in range(1, longest(kind, way) + 1)):
                add_arrived(kind, way, place)
                ring_copy(kind, way, place).start()

    own = rows_at(me, chunk)

    def summed_here(kind):
        acc = part[kind, own].astype(f32)
        for way in (0, 1):
            for distance in range(1, longest(kind, way) + 1):
                if nearer(distance) == 0:
                    ring_copy(kind, way, distance).wait_recv()
                    acc = acc + inbox[kind, way, distance - 1].astype(f32)
        return acc

    both = (hidden, slopes)

    def pass_on(kind, way, distance):
        held = nearer(distance)
        view = both[kind].at[rows_at(beside(1 - way, held), chunk)]
        return remote(
            view, view, ag_send.at[kind, way, distance - 1], ag_recv.at[kind, way, distance - 1],
            wide, beside(way, distance - held),
        )

    def hand_on(kind, way, held):
        for distance in range(1, longest(kind, way) + 1):
            if nearer(distance) == held:
                pass_on(kind, way, distance).start()

    def product(kind, owners):
        spots = [rows_at(owner, chunk) for owner in owners]
        block = jnp.concatenate([both[kind][spot, :ff] for spot in spots], axis=0)
        out = dot(block, down_ref[...]) if kind == 0 else dot_nt(block, up_ref[...])
        out = out.astype(bf16)
        for i, (owner, spot) in enumerate(zip(owners, spots)):
            (out_y, out_g)[kind][spot, :feat] = out[i * chunk : (i + 1) * chunk]
            if kind == 0:
                out_y[spot, feat:] = slopes[spot, ff:]
                for core_to in range(CORES):
                    goal = owner * CORES + core_to
                    at_home = goal == my_far[0]

                    @pl.when(at_home)
                    def _():
                        back_y[rows_at(goal, small)] = out_y[rows_at(goal, small)]

                    @pl.when(jnp.logical_not(at_home))
                    def _():
                        remote(
                            out_y.at[rows_at(goal, small)], back_y.at[rows_at(my_far[0], small)],
                            st_send.at[2, 0, 0], st_recv.at[2, 0, 0],
                            wide_of(owner, my_z, core_to), me,
                        ).start()

    pre = summed_here(0)
    sig = 1.0 / (1.0 + jnp.exp(-pre))
    hidden_own = (pre * sig).astype(bf16)
    hidden[own] = hidden_own
    for way in (0, 1):
        hand_on(0, way, 0)
    slope = sig * (1.0 + pre * (1.0 - sig))
    grad = summed_here(1)
    slopes[own, :ff] = (grad * slope).astype(bf16)
    score_own = jnp.sum(hidden_own.astype(f32) * grad, axis=1, keepdims=True)
    slopes[own, ff:] = jnp.broadcast_to(score_own, (chunk, SIDE_COLS)).astype(bf16)
    for way in (1, 0):
        hand_on(1, way, 0)
    for kind in (0, 1):
        product(kind, [me])
    steps = sorted({nearer(d) for d in range(1, half + 1)})
    for held in steps:
        for kind in (0, 1):
            for way in (0, 1):
                for distance in range(1, longest(kind, way) + 1):
                    if nearer(distance) == held:
                        pass_on(kind, way, distance).wait_recv()
                        hand_on(kind, way, distance)
        for kind in (0, 1):
            product(kind, [
                beside(1 - way, distance)
                for way in (0, 1)
                for distance in range(1, longest(kind, way) + 1)
                if nearer(distance) == held
            ])

    for h, cols in enumerate(halves):
        leave_g[:, cols] = dot(orders[1], out_g[:, cols]).astype(bf16)
        far_stage(2, 1, h, leave_g, back_g, cols)
    landed(2, 0, 0, back_y, small, all_cols)
    back_turn_y[...] = dot(orders[2], back_y[...]).astype(bf16)
    near_stage(3, 0, 0, back_turn_y, home_y, all_cols)
    for h, cols in enumerate(halves):
        landed(2, 1, h, back_g, small, cols)
        back_turn_g[:, cols] = dot(orders[2], back_g[:, cols]).astype(bf16)
        near_stage(3, 1, h, back_turn_g, home_g, cols)

    landed(3, 0, 0, home_y, big, all_cols)
    mine, weighted, named = routes[0]
    mixed_ref[...] = dot(weighted, home_y[:, :feat]).astype(bf16)
    scores_back = home_y[:, feat:]
    lane_of = lax.broadcasted_iota(jnp.int32, (toks, SIDE_COLS), 1)
    row_of = lax.broadcasted_iota(jnp.int32, (toks, SIDE_COLS), 0)
    pick_of = lax.broadcasted_iota(jnp.int32, (picks, SIDE_COLS), 0)
    packed = jnp.zeros((picks, SIDE_COLS), f32)
    for j in range(picks):
        score = dot(jnp.where(named[j], mine, 0.0).astype(bf16), scores_back)
        score = jnp.sum(jnp.where(lane_of == row_of, score, 0.0), axis=0, keepdims=True)
        packed = jnp.where(pick_of == j, score, packed)
    picked = packed[:, :toks]
    mean_score = jnp.sum(weights * picked, axis=0, keepdims=True) / SCALE
    lgrad_ref[...] = (
        row_advantage * (SCALE / total) * (picked - mean_score) * scores * (1.0 - scores)
    )
    for h, cols in enumerate(halves):
        landed(3, 1, h, home_g, big, cols)
    tgrad_ref[...] = (advantage * dot(routes[1][1], home_g[...])).astype(bf16)

    for h, cols in enumerate(halves):
        for stream in range(2):
            gone(0, stream, h, sends[stream], big, cols)
            gone(1, stream, h, turns[stream], small, cols)
        gone(2, 1, h, leave_g, small, cols)
        gone(3, 1, h, back_turn_g, big, cols)
    gone(2, 0, 0, out_y, small, all_cols)
    gone(3, 0, 0, back_turn_y, big, all_cols)
    for kind in (0, 1):
        for way in (0, 1):
            for distance in range(1, longest(kind, way) + 1):
                ring_copy(kind, way, distance).wait_send()
                pass_on(kind, way, distance).wait_send()


def solution(mesh):
    ring = mesh.shape["narrow"]
    side = math.isqrt(mesh.shape["wide"] // CORES)

    def step(tokens, cotangent, gate, groups, ids, advantages, up, down):
        toks, feat = tokens.shape
        ff = up.shape[2]
        rows = mesh.shape["wide"] * SLOTS
        half = ring // 2
        vmem = pl.BlockSpec(memory_space=pltpu.VMEM)
        hbm = pl.BlockSpec(memory_space=pltpu.HBM)
        dma = pltpu.SemaphoreType.DMA
        mixed, token_grad, logit_grad = pl.pallas_call(
            functools.partial(kernel, side, ring),
            out_shape=(
                pltpu.VMEM((toks, feat), bf16),
                pltpu.VMEM((toks, feat), bf16),
                pltpu.VMEM(gate.shape[::-1], f32),
            ),
            in_specs=[hbm] * 8,
            out_specs=[vmem] * 3,
            scratch_shapes=[
                pltpu.VMEM((toks, feat), bf16),
                pltpu.VMEM((toks, feat), bf16),
                pltpu.VMEM(gate.shape[::-1], f32),
                pltpu.VMEM(gate.shape[::-1], jnp.int32),
                pltpu.VMEM((1, toks), jnp.int32),
                pltpu.VMEM((1, advantages.shape[0]), f32),
                pltpu.VMEM((feat, ff), bf16),
                pltpu.VMEM((ff, feat), bf16),
                *[pltpu.VMEM((rows, feat), bf16)] * 9,
                pltpu.VMEM((2, rows, ff), bf16),
                pltpu.VMEM((2, 2, half, rows // ring, ff), bf16),
                pltpu.VMEM((rows, ff), bf16),
                pltpu.VMEM((rows, ff + SIDE_COLS), bf16),
                *[pltpu.VMEM((rows, feat + extra), bf16) for extra in (
                    SIDE_COLS, 0, 0, SIDE_COLS, 0, SIDE_COLS, 0, SIDE_COLS, 0,
                )],
                pltpu.VMEM((3, rows, rows), bf16),
                dma((8,)),
                dma((4, 2, 2)),
                dma((4, 2, 2)),
                dma((2, 2, half)),
                dma((2, 2, half)),
                dma((2, 2, half)),
                dma((2, 2, half)),
            ],
            compiler_params=pltpu.CompilerParams(
                collective_id=0, has_side_effects=True, vmem_limit_bytes=62 * 1024 * 1024
            ),
            cost_estimate=pl.CostEstimate(
                flops=8 * rows * feat * ff, bytes_accessed=4 * feat * ff, transcendentals=0
            ),
        )(
            tokens, cotangent, gate.T, groups.T, ids.reshape(1, toks), advantages.reshape(1, -1), up, down
        )
        return mixed, token_grad, logit_grad.T

    in_specs = (
        P("wide", "narrow"),
        P("wide", "narrow"),
        P("wide", None),
        P("wide", None),
        P("wide"),
        P(),
        P("wide", "narrow", None),
        P("wide", None, "narrow"),
    )
    out_specs = (P("wide", "narrow"), P("wide", "narrow"), P("wide", None))
    return jax.shard_map(step, mesh=mesh, in_specs=in_specs, out_specs=out_specs, check_vma=False)
```

```python
import functools
import math

import jax
import jax.numpy as jnp
from jax import lax
from jax.experimental import pallas as pl
from jax.experimental.pallas import tpu as pltpu
from jax.sharding import PartitionSpec as P

MESH = pl.DeviceIdType.MESH
f32, bf16 = jnp.float32, jnp.bfloat16
SCALE = 2.5
CORES = 2
SLOTS = 2
SIDE_COLS = 128


def dot(a, b):
    return lax.dot_general(a, b, (((1,), (0,)), ((), ())), preferred_element_type=f32)


def dot_nt(a, b):
    return lax.dot_general(a, b, (((1,), (1,)), ((), ())), preferred_element_type=f32)


def dot_tn(a, b):
    return lax.dot_general(a, b, (((0,), (0,)), ((), ())), preferred_element_type=f32)


def rows_at(index, size):
    return pl.ds(pl.multiple_of(index * size, size), size)


def kernel(
    side, ring,
    tok_hbm, cot_hbm, gate_hbm, group_hbm, id_hbm, adv_hbm, up_hbm, down_hbm,
    mixed_ref, tgrad_ref, lgrad_ref,
    tok_ref, cot_ref, gate_ref, group_ref, id_ref, adv_ref, up_ref, down_ref,
    send_x, send_c, mid_x, mid_c, turn_x, turn_c, land_x, land_c, crossed, part, inbox, hidden, slopes,
    out_y, out_g, leave_g, back_y, back_g, back_turn_y, back_turn_g, home_y, home_g, orders,
    w_sem, st_send, st_recv, ring_send, ring_recv, ag_send, ag_recv,
):
    wide, me = lax.axis_index("wide"), lax.axis_index("narrow")
    my_y = lax.div(wide, side * CORES)
    my_z = lax.rem(lax.div(wide, CORES), side)
    my_c = lax.rem(wide, CORES)
    toks, feat = tok_ref.shape
    rows = send_x.shape[0]
    ff = up_ref.shape[1]
    big, small = rows // side, rows // (side * CORES)
    chunk = rows // ring
    half = ring // 2
    all_cols = pl.ds(0, feat + SIDE_COLS)
    halves = [pl.ds(i * (feat // 4), feat // 4) for i in range(4)]
    def nearer(distance):
        return half - 2 if distance == half >= 3 else distance - 1

    hops = {distance - nearer(distance) for distance in range(1, half + 1)}

    def wide_of(y, z, c):
        return (y * side + z) * CORES + c

    def near(stream, k):
        if stream == 0:
            spot = lax.rem(my_z + k, side)
            return spot, wide_of(my_y, spot, my_c)
        spot = lax.rem(my_y + k, side)
        return spot, wide_of(spot, my_z, my_c)

    def far(stream, k):
        if stream == 0:
            spot = lax.rem(my_y * CORES + my_c + k, side * CORES)
            return spot, wide_of(lax.div(spot, CORES), my_z, lax.rem(spot, CORES))
        spot = lax.rem(my_z * CORES + my_c + k, side * CORES)
        return spot, wide_of(my_y, lax.div(spot, CORES), lax.rem(spot, CORES))

    my_near = (my_z, my_y)
    my_far = (my_y * CORES + my_c, my_z * CORES + my_c)

    loads = [
        pltpu.make_async_copy(source, target, w_sem.at[i])
        for i, (source, target) in enumerate((
            (group_hbm, group_ref), (gate_hbm, gate_ref), (tok_hbm, tok_ref), (cot_hbm, cot_ref),
            (id_hbm, id_ref), (adv_hbm, adv_ref), (up_hbm.at[0], up_ref), (down_hbm.at[0], down_ref),
        ))
    ]
    up_copy, down_copy = loads[6:]
    for load in loads:
        load.start()

    barrier = pltpu.get_barrier_semaphore()

    def greet(target, narrow):
        pl.semaphore_signal(barrier, inc=1, device_id=(target, narrow), device_id_type=MESH)

    @pl.loop(1, side * CORES)
    def _(k):
        greet(far(1, k)[1], me)

    @pl.loop(1, side)
    def _(k):
        spot = lax.rem(my_y + k, side)
        greet(wide_of(spot, my_z, 0), me)
        greet(wide_of(spot, my_z, 1), me)

    offsets = sorted({hop for hop in hops} | {ring - hop for hop in hops})
    for offset in offsets:
        greet(wide, lax.rem(me + offset, ring))

    greeted = side * CORES - 1 + (side - 1) * CORES + len(offsets)

    for load in loads[:6]:
        load.wait()

    picks = group_ref.shape[0]
    scores = 1.0 / (1.0 + jnp.exp(-gate_ref[...]))
    total = jnp.sum(scores, axis=0, keepdims=True)
    weights = SCALE * scores / total
    square = lax.broadcasted_iota(jnp.int32, (toks, toks), 0) == lax.broadcasted_iota(
        jnp.int32, (toks, toks), 1
    )

    def column(row):
        return jnp.sum(jnp.where(square, row, 0.0), axis=1, keepdims=True)

    groups = [column(group_ref[j : j + 1].astype(f32)).astype(jnp.int32) for j in range(picks)]
    weight = [column(weights[j : j + 1]) for j in range(picks)]
    lane = lax.broadcasted_iota(jnp.int32, (toks, rows), 1)
    pair = lane >> 1
    core, spot = pair & 1, pair >> 1
    slot = (lane & 1).astype(f32)
    first, second = spot // side, spot % side
    group_of = (wide_of(second, first, core), pair)
    earlier = (
        lax.broadcasted_iota(jnp.int32, (toks, toks), 1)
        < lax.broadcasted_iota(jnp.int32, (toks, toks), 0)
    ).astype(bf16)

    def route(stream):
        named = [groups[j] == group_of[stream] for j in range(picks)]
        hit = functools.reduce(jnp.logical_or, named).astype(f32)
        rank = dot(earlier, hit.astype(bf16))
        mine = jnp.where(rank == slot, hit, 0.0)
        weighted = sum(jnp.where(named[j], weight[j], 0.0) for j in range(picks))
        return mine, (mine * weighted).astype(bf16), named

    sources = (tok_ref, cot_ref)
    routes = []

    def pack(stream):
        routes.append(route(stream))
        sends[stream][...] = dot_tn(routes[stream][0].astype(bf16), sources[stream][...]).astype(bf16)

    def swap(forward):
        i = lax.broadcasted_iota(jnp.int32, (rows, rows), 0)
        j = lax.broadcasted_iota(jnp.int32, (rows, rows), 1)
        out, source = (i, j) if forward else (j, i)
        s, b, c, a = out & 1, (out >> 1) % side, (out >> 1) // side % CORES, (out >> 1) // (side * CORES)
        return (source == ((b * side + a) * CORES + c) * SLOTS + s).astype(bf16)

    def cross():
        i = lax.broadcasted_iota(jnp.int32, (rows, rows), 0)
        j = lax.broadcasted_iota(jnp.int32, (rows, rows), 1)
        s, b, c, a = i & 1, (i >> 1) % side, (i >> 1) // side % CORES, (i >> 1) // (side * CORES)
        return (j == ((b * CORES + c) * side + a) * SLOTS + s).astype(bf16)

    def remote(src, dst, s_sem, r_sem, target, narrow):
        return pltpu.make_async_remote_copy(
            src_ref=src, dst_ref=dst, send_sem=s_sem, recv_sem=r_sem,
            device_id=(target, narrow), device_id_type=MESH,
        )

    def farthest_first(size, k):
        hop = lax.div(k + 1, 2)
        return size // 2 + hop * (1 - 2 * lax.rem(k, 2))

    def near_stage(stage, stream, half_of, src, dst, cols):
        mine = my_near[stream]

        @pl.loop(0, side - 1)
        def _(k):
            spot, target = near(stream, farthest_first(side, k))
            remote(
                src.at[rows_at(spot, big), cols], dst.at[rows_at(mine, big), cols],
                st_send.at[stage, stream, half_of], st_recv.at[stage, stream, half_of], target, me,
            ).start()

        dst[rows_at(mine, big), cols] = src[rows_at(mine, big), cols]

    def far_stage(stage, stream, half_of, src, dst, cols):
        mine = my_far[stream]

        @pl.loop(0, side * CORES - 1)
        def _(k):
            spot, target = far(stream, farthest_first(side * CORES, k))
            remote(
                src.at[rows_at(spot, small), cols], dst.at[rows_at(mine, small), cols],
                st_send.at[stage, stream, half_of], st_recv.at[stage, stream, half_of], target, me,
            ).start()

        dst[rows_at(mine, small), cols] = src[rows_at(mine, small), cols]

    def landed(stage, stream, half_of, dst, part_of, cols):
        view = dst.at[pl.ds(0, rows - part_of), cols]
        pltpu.make_async_copy(view, view, st_recv.at[stage, stream, half_of]).wait()

    def gone(stage, stream, half_of, src, part_of, cols):
        view = src.at[pl.ds(0, rows - part_of), cols]
        pltpu.make_async_copy(view, view, st_send.at[stage, stream, half_of]).wait()

    sends, mids, turns, lands = (send_x, send_c), (mid_x, mid_c), (turn_x, turn_c), (land_x, land_c)
    pack(0)
    pl.semaphore_wait(barrier, greeted)
    for stream in range(2):
        if stream == 1:
            pack(1)
        for h, cols in enumerate(halves):
            near_stage(0, stream, h, sends[stream], mids[stream], cols)
    orders[0] = swap(True)
    orders[1] = cross()
    orders[2] = swap(False)
    id_column = column(id_ref[...].astype(f32))
    samples = adv_ref.shape[1]
    match = id_column == lax.broadcasted_iota(jnp.int32, (toks, samples), 1).astype(f32)
    advantage = jnp.sum(jnp.where(match, adv_ref[...], 0.0), axis=1, keepdims=True)
    row_advantage = jnp.sum(jnp.where(square, advantage, 0.0), axis=0, keepdims=True)
    for h, cols in enumerate(halves):
        for stream in range(2):
            landed(0, stream, h, mids[stream], big, cols)
            turns[stream][:, cols] = dot(orders[0], mids[stream][:, cols]).astype(bf16)
            far_stage(1, stream, h, turns[stream], lands[stream], cols)

    def longest(kind, way):
        return half if kind == way else half - 1

    def beside(way, hops):
        return lax.rem(me + (hops if way == 0 else ring - hops), ring)

    def ring_copy(kind, way, distance):
        owner = beside(way, distance)
        return remote(
            part.at[kind, rows_at(owner, chunk)], inbox.at[kind, way, distance - 1],
            ring_send.at[kind, way, distance - 1], ring_recv.at[kind, way, distance - 1],
            wide, beside(way, distance - nearer(distance)),
        )

    def add_arrived(kind, way, place):
        spot = rows_at(beside(way, place), chunk)
        acc = part[kind, spot].astype(f32)
        for distance in range(1, longest(kind, way) + 1):
            if nearer(distance) == place:
                ring_copy(kind, way, distance).wait_recv()
                acc = acc + inbox[kind, way, distance - 1].astype(f32)
        part[kind, spot] = acc.astype(bf16)

    def starts(kind, way):
        reach = range(1, longest(kind, way) + 1)
        return [d for d in reach if not any(nearer(other) == d for other in reach)]

    def set_off(kind):
        for way in (0, 1):
            for distance in starts(kind, way):
                ring_copy(kind, way, distance).start()

    tile = min(256, ff)
    early = sorted({
        (distance if way == 0 else ring - distance) % ring
        for kind in (0, 1) for way in (0, 1) for distance in starts(kind, way)
    })
    late = [offset for offset in range(ring) if offset not in early]

    def partial(kind, offsets_of):
        spots = [rows_at(lax.rem(me + offset, ring), chunk) for offset in offsets_of]
        source = crossed if kind else land_x
        block = jnp.concatenate([source[spot] for spot in spots], axis=0)

        @pl.loop(0, ff // tile)
        def _(n):
            cols = pl.ds(pl.multiple_of(n * tile, tile), tile)
            out = dot_nt(block, down_ref[cols, :]) if kind else dot(block, up_ref[:, cols])
            out = out.astype(bf16)
            for i, spot in enumerate(spots):
                part[kind, spot, cols] = out[i * chunk : (i + 1) * chunk]

    up_copy.wait()
    for h, cols in enumerate(halves):
        landed(1, 0, h, land_x, small, cols)
    partial(0, early)
    set_off(0)
    down_copy.wait()
    for h, cols in enumerate(halves):
        landed(1, 1, h, land_c, small, cols)
    crossed[...] = dot(orders[1], land_c[...]).astype(bf16)
    partial(1, early)
    set_off(1)
    if late:
        partial(0, late)
        partial(1, late)
    for place in range(half - 1, 0, -1):
        for kind, way in ((0, 0), (0, 1), (1, 1), (1, 0)):
            if any(nearer(d) == place for d in range(1, longest(kind, way) + 1)):
                add_arrived(kind, way, place)
                ring_copy(kind, way, place).start()

    own = rows_at(me, chunk)

    def summed_here(kind):
        acc = part[kind, own].astype(f32)
        for way in (0, 1):
            for distance in range(1, longest(kind, way) + 1):
                if nearer(distance) == 0:
                    ring_copy(kind, way, distance).wait_recv()
                    acc = acc + inbox[kind, way, distance - 1].astype(f32)
        return acc

    both = (hidden, slopes)

    def pass_on(kind, way, distance):
        held = nearer(distance)
        view = both[kind].at[rows_at(beside(1 - way, held), chunk)]
        return remote(
            view, view, ag_send.at[kind, way, distance - 1], ag_recv.at[kind, way, distance - 1],
            wide, beside(way, distance - held),
        )

    def hand_on(kind, way, held):
        for distance in range(1, longest(kind, way) + 1):
            if nearer(distance) == held:
                pass_on(kind, way, distance).start()

    def product(kind, owners):
        spots = [rows_at(owner, chunk) for owner in owners]
        block = jnp.concatenate([both[kind][spot, :ff] for spot in spots], axis=0)
        out = dot(block, down_ref[...]) if kind == 0 else dot_nt(block, up_ref[...])
        out = out.astype(bf16)
        for i, (owner, spot) in enumerate(zip(owners, spots)):
            (out_y, out_g)[kind][spot, :feat] = out[i * chunk : (i + 1) * chunk]
            if kind == 0:
                out_y[spot, feat:] = slopes[spot, ff:]
                for core_to in range(CORES):
                    goal = owner * CORES + core_to
                    at_home = goal == my_far[0]

                    @pl.when(at_home)
                    def _():
                        back_y[rows_at(goal, small)] = out_y[rows_at(goal, small)]

                    @pl.when(jnp.logical_not(at_home))
                    def _():
                        remote(
                            out_y.at[rows_at(goal, small)], back_y.at[rows_at(my_far[0], small)],
                            st_send.at[2, 0, 0], st_recv.at[2, 0, 0],
                            wide_of(owner, my_z, core_to), me,
                        ).start()

    pre = summed_here(0)
    sig = 1.0 / (1.0 + jnp.exp(-pre))
    hidden_own = (pre * sig).astype(bf16)
    hidden[own] = hidden_own
    for way in (0, 1):
        hand_on(0, way, 0)
    slope = sig * (1.0 + pre * (1.0 - sig))
    grad = summed_here(1)
    slopes[own, :ff] = (grad * slope).astype(bf16)
    score_own = jnp.sum(hidden_own.astype(f32) * grad, axis=1, keepdims=True)
    slopes[own, ff:] = jnp.broadcast_to(score_own, (chunk, SIDE_COLS)).astype(bf16)
    for way in (1, 0):
        hand_on(1, way, 0)
    for kind in (0, 1):
        product(kind, [me])
    steps = sorted({nearer(d) for d in range(1, half + 1)})
    for held in steps:
        for kind in (0, 1):
            for way in (0, 1):
                for distance in range(1, longest(kind, way) + 1):
                    if nearer(distance) == held:
                        pass_on(kind, way, distance).wait_recv()
                        hand_on(kind, way, distance)
        for kind in (0, 1):
            product(kind, [
                beside(1 - way, distance)
                for way in (0, 1)
                for distance in range(1, longest(kind, way) + 1)
                if nearer(distance) == held
            ])

    for h, cols in enumerate(halves):
        leave_g[:, cols] = dot(orders[1], out_g[:, cols]).astype(bf16)
        far_stage(2, 1, h, leave_g, back_g, cols)
    landed(2, 0, 0, back_y, small, all_cols)
    back_turn_y[...] = dot(orders[2], back_y[...]).astype(bf16)
    near_stage(3, 0, 0, back_turn_y, home_y, all_cols)
    for h, cols in enumerate(halves):
        landed(2, 1, h, back_g, small, cols)
        back_turn_g[:, cols] = dot(orders[2], back_g[:, cols]).astype(bf16)
        near_stage(3, 1, h, back_turn_g, home_g, cols)

    landed(3, 0, 0, home_y, big, all_cols)
    mine, weighted, named = routes[0]
    mixed_ref[...] = dot(weighted, home_y[:, :feat]).astype(bf16)
    scores_back = home_y[:, feat:]
    lane_of = lax.broadcasted_iota(jnp.int32, (toks, SIDE_COLS), 1)
    row_of = lax.broadcasted_iota(jnp.int32, (toks, SIDE_COLS), 0)
    pick_of = lax.broadcasted_iota(jnp.int32, (picks, SIDE_COLS), 0)
    packed = jnp.zeros((picks, SIDE_COLS), f32)
    for j in range(picks):
        score = dot(jnp.where(named[j], mine, 0.0).astype(bf16), scores_back)
        score = jnp.sum(jnp.where(lane_of == row_of, score, 0.0), axis=0, keepdims=True)
        packed = jnp.where(pick_of == j, score, packed)
    picked = packed[:, :toks]
    mean_score = jnp.sum(weights * picked, axis=0, keepdims=True) / SCALE
    lgrad_ref[...] = (
        row_advantage * (SCALE / total) * (picked - mean_score) * scores * (1.0 - scores)
    )
    for h, cols in enumerate(halves):
        landed(3, 1, h, home_g, big, cols)
    tgrad_ref[...] = (advantage * dot(routes[1][1], home_g[...])).astype(bf16)

    for h, cols in enumerate(halves):
        for stream in range(2):
            gone(0, stream, h, sends[stream], big, cols)
            gone(1, stream, h, turns[stream], small, cols)
        gone(2, 1, h, leave_g, small, cols)
        gone(3, 1, h, back_turn_g, big, cols)
    gone(2, 0, 0, out_y, small, all_cols)
    gone(3, 0, 0, back_turn_y, big, all_cols)
    for kind in (0, 1):
        for way in (0, 1):
            for distance in range(1, longest(kind, way) + 1):
                ring_copy(kind, way, distance).wait_send()
                pass_on(kind, way, distance).wait_send()


def solution(mesh):
    ring = mesh.shape["narrow"]
    side = math.isqrt(mesh.shape["wide"] // CORES)

    def step(tokens, cotangent, gate, groups, ids, advantages, up, down):
        toks, feat = tokens.shape
        ff = up.shape[2]
        rows = mesh.shape["wide"] * SLOTS
        half = ring // 2
        vmem = pl.BlockSpec(memory_space=pltpu.VMEM)
        hbm = pl.BlockSpec(memory_space=pltpu.HBM)
        dma = pltpu.SemaphoreType.DMA
        mixed, token_grad, logit_grad = pl.pallas_call(
            functools.partial(kernel, side, ring),
            out_shape=(
                pltpu.VMEM((toks, feat), bf16),
                pltpu.VMEM((toks, feat), bf16),
                pltpu.VMEM(gate.shape[::-1], f32),
            ),
            in_specs=[hbm] * 8,
            out_specs=[vmem] * 3,
            scratch_shapes=[
                pltpu.VMEM((toks, feat), bf16),
                pltpu.VMEM((toks, feat), bf16),
                pltpu.VMEM(gate.shape[::-1], f32),
                pltpu.VMEM(gate.shape[::-1], jnp.int32),
                pltpu.VMEM((1, toks), jnp.int32),
                pltpu.VMEM((1, advantages.shape[0]), f32),
                pltpu.VMEM((feat, ff), bf16),
                pltpu.VMEM((ff, feat), bf16),
                *[pltpu.VMEM((rows, feat), bf16)] * 9,
                pltpu.VMEM((2, rows, ff), bf16),
                pltpu.VMEM((2, 2, half, rows // ring, ff), bf16),
                pltpu.VMEM((rows, ff), bf16),
                pltpu.VMEM((rows, ff + SIDE_COLS), bf16),
                *[pltpu.VMEM((rows, feat + extra), bf16) for extra in (
                    SIDE_COLS, 0, 0, SIDE_COLS, 0, SIDE_COLS, 0, SIDE_COLS, 0,
                )],
                pltpu.VMEM((3, rows, rows), bf16),
                dma((8,)),
                dma((4, 2, 4)),
                dma((4, 2, 4)),
                dma((2, 2, half)),
                dma((2, 2, half)),
                dma((2, 2, half)),
                dma((2, 2, half)),
            ],
            compiler_params=pltpu.CompilerParams(
                collective_id=0, has_side_effects=True, vmem_limit_bytes=62 * 1024 * 1024
            ),
            cost_estimate=pl.CostEstimate(
                flops=8 * rows * feat * ff, bytes_accessed=4 * feat * ff, transcendentals=0
            ),
        )(
            tokens, cotangent, gate.T, groups.T, ids.reshape(1, toks), advantages.reshape(1, -1), up, down
        )
        return mixed, token_grad, logit_grad.T

    in_specs = (
        P("wide", "narrow"),
        P("wide", "narrow"),
        P("wide", None),
        P("wide", None),
        P("wide"),
        P(),
        P("wide", "narrow", None),
        P("wide", None, "narrow"),
    )
    out_specs = (P("wide", "narrow"), P("wide", "narrow"), P("wide", None))
    return jax.shard_map(step, mesh=mesh, in_specs=in_specs, out_specs=out_specs, check_vma=False)
```
